32 devices in a mesh: ep: 4 (over y, x), blk: 8 (over z, core).
Axes of the slice: x: 2, y: 2, z: 4, core: 2. Of those that a mesh axis runs over, the one named last changes fastest.
Arguments:
- tokens: bfloat16 [4096, 7168], P(('ep', 'blk')), may hold values from -6 to 6
- route: int32 [4096, 8], P(('ep', 'blk')), may hold values from 0 to 255, as said below
- gates: float32 [4096, 8], P(('ep', 'blk')), may hold values from 0.1 to 1
- cotangent: bfloat16 [4096, 7168], P(('ep', 'blk')), may hold values from -6 to 6
- w_gate: bfloat16 [4, 7168, 2048], P('ep', None, 'blk'), may hold values from -0.0625 to 0.0625
- w_up: bfloat16 [4, 7168, 2048], P('ep', None, 'blk'), may hold values from -0.0625 to 0.0625
- w_down: bfloat16 [4, 2048, 7168], P('ep', 'blk'), may hold values from -0.125 to 0.125
Outputs:
- mixed: bfloat16 [4096, 7168], P(('ep', 'blk'))
- grad_tokens: bfloat16 [4096, 7168], P(('ep', 'blk'))
- grad_gate: bfloat16 [4, 7168, 2048], P('ep', None, 'blk')
- grad_up: bfloat16 [4, 7168, 2048], P('ep', None, 'blk')
- grad_down: bfloat16 [4, 2048, 7168], P('ep', 'blk')
The draws below stay inside these ranges and needn't reach their ends.
Inputs may be any that keep to these rules, and one draw needn't show every extreme that they name: `route`: each row names 8 different experts; numbers below 4 are the window's experts. Among the 128 rows of one device each window expert is named by 1 to 4 rows, and in every draw one window expert is named by exactly 4 rows on every device.
All inputs are finite; a program needn't handle non-finite values.
Results may differ from the reference program's by a relative error of at most 0.025.
Values may be sent and summed in bfloat16 or wider, within the bound.
A program may use at most 192 MiB of HBM per device.

```python
import math
import jax
import jax.numpy as jnp
from jax import lax

D = 7168
FF = 2048
TOP = 8
IDS = 256
TOK_DEV = 128
CAP = 4
EXPERTS = 4
TOKENS = 4096
N_BLK = 8


def draw_route(key, part):
    blocks = TOKENS // TOK_DEV
    key_count, key_full, key_rank, key_other, key_order = jax.random.split(key, 5)
    counts = jax.random.randint(key_count, (blocks, EXPERTS), 1, CAP + 1)
    fullest = jax.random.randint(key_full, (), 0, EXPERTS)
    counts = jnp.where(jnp.arange(EXPERTS)[None, :] == fullest, CAP, counts)
    raw_rank = jax.random.randint(key_rank, (blocks, EXPERTS, TOK_DEV), 0, 1 << 20)
    rank_scores = raw_rank * TOK_DEV + jnp.arange(TOK_DEV)
    sorted_order = jnp.argsort(rank_scores, axis=-1)
    ranks = jnp.argsort(sorted_order, axis=-1)
    member = jnp.transpose(ranks < counts[:, :, None], (0, 2, 1))
    member_all = jnp.pad(member, ((0, 0), (0, 0), (0, IDS - EXPERTS)))
    others = jax.random.randint(key_other, (blocks, TOK_DEV, IDS), 0, 1 << 20) * IDS + jnp.arange(IDS)
    inside = jnp.arange(IDS) < EXPERTS
    window_scores = jnp.where(member_all, (1 << 29) + jnp.arange(IDS), -1 - jnp.arange(IDS))
    scores = jnp.where(inside, window_scores, others)
    chosen_scores, chosen = lax.top_k(scores, TOP)
    shuffle = jax.random.randint(key_order, (blocks, TOK_DEV, TOP), 0, 1 << 20) * TOP + jnp.arange(TOP)
    shuffle_order = jnp.argsort(shuffle, axis=-1)
    ids = jnp.take_along_axis(chosen, shuffle_order, axis=-1)
    return ids.reshape(TOKENS, TOP).astype(jnp.int32)


def levels(own_key, shape, shards, low, largest):
    def one(axis_at, parts):
        draws = jax.random.uniform(jax.random.fold_in(jax.random.fold_in(own_key, 6), axis_at), (parts,), jnp.float32, low / len(shards), largest / len(shards))
        return jnp.repeat(jnp.exp(draws), shape[axis_at] // parts).reshape((-1,) + (1,) * (len(shape) - axis_at - 1))

    level = one(*shards[0])
    for cut in shards[1:]:
        level = level * one(*cut)
    return level


def normal_values(stream_key, dims, spread, limit, cuts=(), kind=jnp.bfloat16):
    values = jax.random.normal(stream_key, dims, jnp.float32) * spread
    if len(cuts) > 0:
        values = levels(stream_key, dims, cuts, -0.22, 0.18) * values
    return jnp.clip(values, min=-limit, max=limit).astype(kind)


def setup_inputs(seed: int = 0) -> dict:
    keys = jax.random.split(jax.random.key(seed), 8)
    return {
        "tokens": normal_values(keys[0], (TOKENS, D), 1.0, 6.0, ((0, 32),)),
        "route": draw_route(jax.random.fold_in(keys[7], 71), 0),
        "gates": jnp.clip(jnp.exp(math.log(1.0) - 2.3025851 * jax.random.uniform(keys[2], (TOKENS, TOP), jnp.float32) ** levels(keys[2], (TOKENS, TOP), ((0, 32),), -0.2, 0.2)), 0.1, 1.0),
        "cotangent": normal_values(keys[3], (TOKENS, D), 1.0, 6.0, ((0, 32),)),
        "w_gate": normal_values(keys[4], (EXPERTS, D, FF), D ** -0.5, 0.0625, ((0, 4), (2, 8))),
        "w_up": normal_values(keys[5], (EXPERTS, D, FF), D ** -0.5, 0.0625, ((0, 4), (2, 8))),
        "w_down": normal_values(keys[6], (EXPERTS, FF, D), FF ** -0.5, 0.125, ((0, 4), (1, 8))),
    }


def routing(route, gates):
    blocks = TOKENS // TOK_DEV
    ids = route.reshape(blocks, TOK_DEV, TOP)
    matches = ids[:, :, :, None] == jnp.arange(EXPERTS, dtype=jnp.int32)
    member = jnp.any(matches, axis=2)
    picks = gates.reshape(blocks, TOK_DEV, TOP)[:, :, :, None]
    weight = jnp.sum(jnp.where(matches, picks, jnp.zeros_like(picks)), axis=2)
    places = jnp.cumsum(member.astype(jnp.int32), axis=1) - 1
    picked = member[..., None] & (places[..., None] == jnp.arange(CAP, dtype=jnp.int32))
    return picked, weight


def expert_pass(operands):
    rows_x, rows_d, gate_w, up_w, down_w = operands
    count_rows = rows_x.shape[0]
    part = FF // N_BLK
    gate_pre = jnp.dot(rows_x, gate_w, preferred_element_type=jnp.float32)
    up_pre = jnp.dot(rows_x, up_w, preferred_element_type=jnp.float32)
    logistic = jax.nn.sigmoid(gate_pre)
    hidden = (gate_pre * logistic * up_pre).astype(jnp.bfloat16)
    hidden_blocks = hidden.reshape(count_rows, N_BLK, part).astype(jnp.float32)
    down_blocks = down_w.reshape(N_BLK, part, D).astype(jnp.float32)
    terms = jnp.einsum('rbf,bfd->brd', hidden_blocks, down_blocks)
    terms = lax.optimization_barrier(terms.astype(jnp.bfloat16)).astype(jnp.float32)
    expert_rows = jnp.sum(terms, axis=0).astype(jnp.bfloat16)
    hidden_grad = jnp.dot(rows_d, down_w.T, preferred_element_type=jnp.float32)
    grad_down = jnp.dot(hidden.T, rows_d, preferred_element_type=jnp.float32).astype(jnp.bfloat16)
    slope = logistic * (1.0 + gate_pre * (1.0 - logistic))
    gate_grad = (hidden_grad * up_pre * slope).astype(jnp.bfloat16)
    up_grad = (hidden_grad * gate_pre * logistic).astype(jnp.bfloat16)
    grad_gate = jnp.dot(rows_x.T, gate_grad, preferred_element_type=jnp.float32).astype(jnp.bfloat16)
    grad_up = jnp.dot(rows_x.T, up_grad, preferred_element_type=jnp.float32).astype(jnp.bfloat16)
    gate_blocks = gate_grad.reshape(count_rows, N_BLK, part).astype(jnp.float32)
    up_blocks = up_grad.reshape(count_rows, N_BLK, part).astype(jnp.float32)
    wg_blocks = gate_w.reshape(D, N_BLK, part).astype(jnp.float32)
    wu_blocks = up_w.reshape(D, N_BLK, part).astype(jnp.float32)
    back = jnp.einsum('rbf,dbf->brd', gate_blocks, wg_blocks) + jnp.einsum('rbf,dbf->brd', up_blocks, wu_blocks)
    back = lax.optimization_barrier(back.astype(jnp.bfloat16)).astype(jnp.float32)
    input_rows = jnp.sum(back, axis=0).astype(jnp.bfloat16)
    return expert_rows, input_rows, grad_gate, grad_up, grad_down


def reference(tokens, route, gates, cotangent, w_gate, w_up, w_down):
    blocks = TOKENS // TOK_DEV
    picked, weight = routing(route, gates)
    picked_f = picked.astype(jnp.float32)
    token_f = tokens.reshape(blocks, TOK_DEV, D).astype(jnp.float32)
    x_slots = jnp.einsum('btec,btd->ebcd', picked_f, token_f).astype(jnp.bfloat16)
    x_slots = x_slots.reshape(EXPERTS, blocks * CAP, D)
    slot_gate = jnp.einsum('btec,bte->ebc', picked_f, weight.astype(jnp.float32))
    cot_f = cotangent.reshape(blocks, TOK_DEV, D).astype(jnp.float32)
    d_slots = (jnp.einsum('btec,btd->ebcd', picked_f, cot_f) * slot_gate[..., None]).astype(jnp.bfloat16)
    d_slots = d_slots.reshape(EXPERTS, blocks * CAP, D)
    expert_rows, input_rows, grad_gate, grad_up, grad_down = lax.map(expert_pass, (x_slots, d_slots, w_gate, w_up, w_down))
    expert_rows = expert_rows.reshape(EXPERTS, blocks, CAP, D).astype(jnp.float32)
    input_rows = input_rows.reshape(EXPERTS, blocks, CAP, D).astype(jnp.float32)
    weighted = picked_f * weight.astype(jnp.float32)[..., None]
    mixed = jnp.einsum('btec,ebcd->btd', weighted, expert_rows, precision=lax.Precision.HIGHEST)
    mixed = mixed.reshape(TOKENS, D).astype(jnp.bfloat16)
    grad_tokens = jnp.einsum('btec,ebcd->btd', picked_f, input_rows, precision=lax.Precision.HIGHEST)
    grad_tokens = grad_tokens.reshape(TOKENS, D).astype(jnp.bfloat16)
    return (mixed, grad_tokens, grad_gate, grad_up, grad_down)
```

```python
import functools

import jax
import jax.numpy as jnp
from jax import lax
from jax.experimental import pallas as pl
from jax.experimental.pallas import tpu as pltpu
from jax.sharding import PartitionSpec as P

CAP = 4
CUTS = 4
ROWS = CAP * CUTS
TILE = 256
F32 = jnp.float32
BF16 = jnp.bfloat16
MESH = pl.DeviceIdType.MESH


def mm(a, b):
    return jnp.dot(a, b, preferred_element_type=F32)


def mm_nt(a, b):
    return lax.dot_general(a, b, (((1,), (1,)), ((), ())), preferred_element_type=F32)


def place(shape, row_dim, q):
    row = lax.broadcasted_iota(jnp.int32, shape, row_dim)
    col = lax.broadcasted_iota(jnp.int32, shape, 1 - row_dim)
    hit = (row // CAP) * ROWS + q * CAP + row % CAP == col
    return jnp.where(hit, 1.0, 0.0).astype(BF16)


def exchange(
    E, L, pq_ref, sg_ref, tok_hbm, cot_hbm, wg_hbm, wu_hbm, wd_hbm,
    bo_hbm, bi_hbm, xo_hbm, do_hbm, h_ref, a_ref, b_ref,
    tok, cot, wg, wu, wd, xs, ds, xin, din, xg, dg, gp, up,
    yp, ysib, yline, yret, bo, qp, qsib, qline, qret, bi,
    load_sem, out_sem, disp_s, disp_r, gat_s, gat_r, sib_s, sib_r, line_s, line_r, ret_s, ret_r,
):
    ep = lax.axis_index("ep")
    blk = lax.axis_index("blk")
    l = blk // 2
    c = blk % 2
    D = tok.shape[1]
    W = D // CUTS
    R = E * CAP
    rows = 2 * L * R
    sibling = {"blk": 2 * l + (1 - c)}
    right = {"blk": blk + 2}
    left = {"blk": blk - 2}
    has_right = l < L - 1
    has_left = l > 0

    loads = [
        pltpu.make_async_copy(s, d, load_sem.at[i])
        for i, (s, d) in enumerate(
            [(tok_hbm, tok), (cot_hbm, cot), (wg_hbm.at[0], wg), (wu_hbm.at[0], wu), (wd_hbm.at[0], wd)]
        )
    ]
    for cp in loads:
        cp.start()

    barrier = pltpu.get_barrier_semaphore()
    for k in range(1, E):
        pl.semaphore_signal(barrier, inc=1, device_id={"ep": lax.rem(ep + k, E)}, device_id_type=MESH)
    pl.semaphore_signal(barrier, inc=1, device_id=sibling, device_id_type=MESH)

    @pl.when(has_right)
    def _():
        pl.semaphore_signal(barrier, inc=1, device_id=right, device_id_type=MESH)

    @pl.when(has_left)
    def _():
        pl.semaphore_signal(barrier, inc=1, device_id=left, device_id_type=MESH)

    ends = jnp.where(l > 0, 1, 0) + jnp.where(l < L - 1, 1, 0)
    pl.semaphore_wait(barrier, E + ends)

    def remote(src, dst, ss, rs, dev):
        return pltpu.make_async_remote_copy(
            src_ref=src, dst_ref=dst, send_sem=ss, recv_sem=rs, device_id=dev, device_id_type=MESH
        )

    tails = []

    def tail(cond, make):
        tails.append((cond, make))

    def ep_copy(n, src, dst, ss, rs, j):
        return remote(src.at[j], dst.at[ep], ss.at[n, j], rs.at[n, ep], {"ep": j})

    def ep_send(n, src, dst, ss, rs):
        for k in range(1, E):
            j = lax.rem(ep + k, E)
            ep_copy(n, src, dst, ss, rs, j).start()
            tail(None, functools.partial(ep_copy, n, src, dst, ss, rs, j))

    def ep_wait(n, src, dst, ss, rs):
        for k in range(1, E):
            j = lax.rem(ep + k, E)
            remote(src.at[j], dst.at[j], ss.at[n, j], rs.at[n, j], {"ep": j}).wait_recv()

    def select(src, dst, own, scale):
        def step(t, carry):
            at = pl.ds(pl.multiple_of(t * TILE, TILE), TILE)
            acc = jnp.zeros((E * ROWS, TILE), F32)
            for q in range(CUTS):
                acc += mm(pq_ref[q], src[:, pl.ds(pl.multiple_of(q * W + t * TILE, TILE), TILE)])
            if scale:
                acc = acc * sg_ref[...]
            dst[:, :, at] = acc.astype(BF16).reshape(E, ROWS, TILE)
            return carry

        lax.fori_loop(0, W // TILE, step, 0)
        own[ep] = dst[ep]

    def settle(src, dst):
        def step(t, carry):
            at = pl.ds(pl.multiple_of(t * TILE, TILE), TILE)
            part = src[:, :, at].reshape(E * ROWS, TILE)
            for q in range(CUTS):
                out = mm(place((R, E * ROWS), 0, q), part)
                dst[blk, :, pl.ds(pl.multiple_of(q * W + t * TILE, TILE), TILE)] = out.astype(BF16)
            return carry

        lax.fori_loop(0, W // TILE, step, 0)

    def g_copy(n, buf, j, way, dev):
        b = 2 * j + c
        return remote(buf.at[b], buf.at[b], gat_s.at[n, way, j], gat_r.at[n, b], dev)

    def g_got(n, buf, b):
        remote(buf.at[b], buf.at[b], gat_s.at[n, 0, 0], gat_r.at[n, b], sibling).wait_recv()

    def guarded(cond, fn):
        if cond is None:
            fn()
        else:
            pl.when(cond)(fn)

    def g_send(n, buf, s):
        steps = []
        if s < L - 1:
            steps += [(has_right & (l - s >= 0), l - s, 0, right), (has_left & (l + s < L), l + s, 1, left)]
        if s == 0:
            steps += [(None, l, 2, sibling)]
        else:
            steps += [(l - s >= 0, l - s, 2, sibling), (l + s < L, l + s, 2, sibling)]
        for cond, j, way, dev in steps:
            guarded(cond, lambda j=j, way=way, dev=dev: g_copy(n, buf, j, way, dev).start())
            tail(cond, functools.partial(g_copy, n, buf, j, way, dev))

    def g_wait(n, buf, s):
        pl.when(l - 1 - s >= 0)(lambda: g_got(n, buf, 2 * (l - 1 - s) + c))
        pl.when(l + 1 + s < L)(lambda: g_got(n, buf, 2 * (l + 1 + s) + c))

    def g_sib(n, buf):
        for j in range(L):
            g_got(n, buf, 2 * j + (1 - c))

    def s_copy(n, part, sib, j):
        return remote(part.at[2 * j + 1 - c], sib.at[j], sib_s.at[n, j], sib_r.at[n, j], sibling)

    def s_send(n, part, sib):
        for j in range(L):
            s_copy(n, part, sib, j).start()
            tail(None, functools.partial(s_copy, n, part, sib, j))

    def s_wait(n, part, sib):
        for j in range(L):
            s_copy(n, part, sib, j).wait_recv()

    def r_copy(n, part, line, j, up_way, dev):
        k = j + up_way
        return remote(part.at[2 * j + c], line.at[k], line_s.at[n, j], line_r.at[n, k], dev)

    def total(part, sib, lines, b, j):
        def step(t, carry):
            at = pl.ds(pl.multiple_of(t * 1024, 1024), 1024)
            acc = part[b, :, at].astype(F32) + sib[j, :, at].astype(F32)
            for line, k in lines:
                acc += line[k, :, at].astype(F32)
            part[b, :, at] = acc.astype(BF16)
            return carry

        lax.fori_loop(0, D // 1024, step, 0)

    def r_step(n, part, sib, line, s):
        jl = s - (L - 1 - l)
        jr = L - 1 - s + l

        def go(j, up_way, dev, first):
            def fn():
                if not first:
                    k = j + up_way
                    r_copy(n, part, line, j, up_way, dev).wait_recv()
                    total(part, sib, [(line, k)], 2 * j + c, j)
                else:
                    total(part, sib, [], 2 * j + c, j)
                r_copy(n, part, line, j, up_way, dev).start()

            return fn

        lw = has_left & (jl >= 0)
        rw = has_right & (jr < L)
        pl.when(lw & (l == L - 1))(go(jl, 0, left, True))
        pl.when(rw & (l == 0))(go(jr, 1, right, True))
        if L > 2:
            pl.when(lw & (l < L - 1))(go(jl, 0, left, False))
            pl.when(rw & (l > 0))(go(jr, 1, right, False))
        tail(lw, functools.partial(r_copy, n, part, line, jl, 0, left))
        tail(rw, functools.partial(r_copy, n, part, line, jr, 1, right))

    def r_last(n, part, sib, line, ret, back):
        def join(line_slots):
            def fn():
                for k in line_slots:
                    remote(part.at[blk], line.at[k], line_s.at[n, 0], line_r.at[n, k], sibling).wait_recv()
                total(part, sib, [(line, k) for k in line_slots], blk, l)

            return fn

        pl.when(l == 0)(join([l]))
        pl.when(l == L - 1)(join([l + 1]))
        if L > 2:
            pl.when((l > 0) & (l < L - 1))(join([l, l + 1]))

        def step(t, carry):
            at = pl.ds(pl.multiple_of(t * TILE, TILE), TILE)
            acc = jnp.zeros((E * ROWS, TILE), F32)
            for q in range(CUTS):
                own = part[blk, :, pl.ds(pl.multiple_of(q * W + t * TILE, TILE), TILE)]
                acc += mm(place((E * ROWS, R), 1, q), own)
            ret[:, :, at] = acc.astype(BF16).reshape(E, ROWS, TILE)
            return carry

        lax.fori_loop(0, W // TILE, step, 0)
        back[ep] = ret[ep]
        ep_send(n, ret, back, ret_s, ret_r)

    loads[0].wait()
    select(tok, xs, xin, False)
    ep_send(0, xs, xin, disp_s, disp_r)
    loads[1].wait()
    select(cot, ds, din, True)
    ep_send(1, ds, din, disp_s, disp_r)
    ep_wait(0, xs, xin, disp_s, disp_r)
    settle(xin, xg)
    g_send(0, xg, 0)
    ep_wait(1, ds, din, disp_s, disp_r)
    settle(din, dg)
    for s in range(1, L):
        g_wait(0, xg, s - 1)
        g_send(0, xg, s)
    g_send(1, dg, 0)
    g_sib(0, xg)
    x_out = pltpu.make_async_copy(xg, xo_hbm, out_sem.at[0])
    x_out.start()
    loads[2].wait()
    loads[3].wait()

    def both(t, carry):
        at = pl.ds(pl.multiple_of(t * W, TILE), W)
        x = xg[:, :, at].reshape(rows, W)
        gp[...] += mm(x, wg[at, :])
        up[...] += mm(x, wu[at, :])
        return carry

    gp[...] = jnp.zeros_like(gp)
    up[...] = jnp.zeros_like(up)
    lax.fori_loop(0, CUTS, both, 0)
    h_ref[...] = (gp[...] * jax.nn.sigmoid(gp[...]) * up[...]).astype(BF16)
    if L > 1:
        g_wait(1, dg, 0)
        g_send(1, dg, 1)
    loads[4].wait()

    def down(t, carry):
        at = pl.ds(pl.multiple_of(t * 512, 512), 512)
        yp[:, :, at] = mm(h_ref[...], wd[:, at]).astype(BF16).reshape(2 * L, R, 512)
        return carry

    lax.fori_loop(0, D // 512, down, 0)
    s_send(0, yp, ysib)
    if L > 2:
        g_wait(1, dg, 1)
        g_send(1, dg, 2)
    s_wait(0, yp, ysib)
    r_step(0, yp, ysib, yline, 0)
    for s in range(3, L):
        g_wait(1, dg, s - 1)
        g_send(1, dg, s)
        r_step(0, yp, ysib, yline, s - 2)
    g_sib(1, dg)
    d_out = pltpu.make_async_copy(dg, do_hbm, out_sem.at[1])
    d_out.start()

    hg = jnp.zeros((rows, gp.shape[1]), F32)

    def pull(t, carry):
        at = pl.ds(pl.multiple_of(t * W, TILE), W)
        return carry + mm_nt(dg[:, :, at].reshape(rows, W), wd[:, at])

    hg = lax.fori_loop(0, CUTS, pull, hg)
    g = gp[...]
    u = up[...]
    sig = jax.nn.sigmoid(g)
    a_ref[...] = (hg * u * (sig * (1.0 + g * (1.0 - sig)))).astype(BF16)
    b_ref[...] = (hg * g * sig).astype(BF16)
    done = max(1, L - 2)
    if done < L - 1:
        r_step(0, yp, ysib, yline, done)

    def back_rows(t, carry):
        at = pl.ds(pl.multiple_of(t * 512, 512), 512)
        q = mm_nt(a_ref[...], wg[at, :]) + mm_nt(b_ref[...], wu[at, :])
        qp[:, :, at] = q.astype(BF16).reshape(2 * L, R, 512)
        return carry

    lax.fori_loop(0, D // 512, back_rows, 0)
    s_send(1, qp, qsib)
    s_wait(1, qp, qsib)
    r_step(1, qp, qsib, qline, 0)
    r_last(0, yp, ysib, yline, yret, bo)
    for s in range(1, L - 1):
        r_step(1, qp, qsib, qline, s)
    ep_wait(0, yret, bo, ret_s, ret_r)
    o_out = pltpu.make_async_copy(bo, bo_hbm, out_sem.at[2])
    o_out.start()
    r_last(1, qp, qsib, qline, qret, bi)
    ep_wait(1, qret, bi, ret_s, ret_r)
    i_out = pltpu.make_async_copy(bi, bi_hbm, out_sem.at[3])
    i_out.start()
    for cond, make in tails:
        guarded(cond, lambda make=make: make().wait_send())
    for cp in (x_out, d_out, o_out, i_out):
        cp.wait()


def combine(pw_ref, pt_ref, bo_ref, bi_ref, mixed_ref, grad_ref):
    e_rows = bo_ref.shape[0] * ROWS
    width = bo_ref.shape[2]
    y = bo_ref[...].reshape(e_rows, width)
    mixed_ref[...] = (mm(pw_ref[0, 0], y) + mm(pw_ref[1, 0], y)).astype(BF16)
    grad_ref[...] = mm(pt_ref[0], bi_ref[...].reshape(e_rows, width)).astype(BF16)


def local(tokens, route, gates, cotangent, w_gate, w_up, w_down):
    E = lax.axis_size("ep")
    L = lax.axis_size("blk") // 2
    T, D = tokens.shape
    W = D // CUTS
    R = E * CAP
    rows = 2 * L * R
    F = w_gate.shape[2]
    matches = route[:, :, None] == jnp.arange(E, dtype=jnp.int32)
    member = jnp.any(matches, axis=1)
    weight = jnp.sum(jnp.where(matches, gates[:, :, None], 0.0), axis=1)
    earlier = jnp.tril(jnp.ones((T, T), BF16), -1)
    places = mm(earlier, member.astype(BF16)).astype(jnp.int32)
    picked = member[:, :, None] & (places[:, :, None] == jnp.arange(CAP, dtype=jnp.int32))
    picked_w = jnp.where(picked, weight[:, :, None], 0.0)
    slot_gate = jnp.sum(picked_w, axis=0)
    sg = jnp.broadcast_to(slot_gate[:, None, :], (E, CUTS, CAP)).reshape(E * ROWS, 1)
    quarter = jnp.eye(CUTS, dtype=bool)[:, None, None, :, None]

    def spread(m):
        wide = jnp.where(quarter, m[None, :, :, None, :], jnp.zeros((), m.dtype))
        return wide.reshape(CUTS, T, E * ROWS)

    pt = spread(picked.astype(BF16))
    pq = pt.transpose(0, 2, 1)
    hi = picked_w.astype(BF16)
    lo = (picked_w - hi.astype(F32)).astype(BF16)
    pw = jnp.stack([spread(hi), spread(lo)])

    vm = pl.BlockSpec(memory_space=pltpu.VMEM)
    hbm = pl.BlockSpec(memory_space=pl.ANY)
    sds = jax.ShapeDtypeStruct
    msg = pltpu.VMEM((E, ROWS, W), BF16)
    allrows = pltpu.VMEM((2 * L, R, D), BF16)
    own = pltpu.VMEM((L, R, D), BF16)
    line = pltpu.VMEM((L + 1, R, D), BF16)
    dma = pltpu.SemaphoreType.DMA
    bo, bi, rows_x, rows_d, hidden, gate_grad, up_grad = pl.pallas_call(
        functools.partial(exchange, E, L),
        out_shape=(
            sds((E, ROWS, W), BF16),
            sds((E, ROWS, W), BF16),
            sds((2 * L, R, D), BF16),
            sds((2 * L, R, D), BF16),
            sds((rows, F), BF16),
            sds((rows, F), BF16),
            sds((rows, F), BF16),
        ),
        in_specs=[vm, vm, hbm, hbm, hbm, hbm, hbm],
        out_specs=(hbm, hbm, hbm, hbm, vm, vm, vm),
        scratch_shapes=[
            pltpu.VMEM((T, D), BF16),
            pltpu.VMEM((T, D), BF16),
            pltpu.VMEM((D, F), BF16),
            pltpu.VMEM((D, F), BF16),
            pltpu.VMEM((F, D), BF16),
            msg, msg, msg, msg,
            allrows, allrows,
            pltpu.VMEM((rows, F), F32),
            pltpu.VMEM((rows, F), F32),
            allrows, own, line, msg, msg,
            allrows, own, line, msg, msg,
            dma((5,)),
            dma((4,)),
            dma((2, E)),
            dma((2, E)),
            dma((2, 3, L)),
            dma((2, 2 * L)),
            dma((2, L)),
            dma((2, L)),
            dma((2, L)),
            dma((2, L + 1)),
            dma((2, E)),
            dma((2, E)),
        ],
        compiler_params=pltpu.CompilerParams(
            collective_id=0, has_side_effects=True, vmem_limit_bytes=60 * 1024 * 1024
        ),
    )(pq, sg, tokens, cotangent, w_gate, w_up, w_down)

    mixed, grad_tokens = pl.pallas_call(
        combine,
        grid=(CUTS,),
        out_shape=(sds((T, D), BF16), sds((T, D), BF16)),
        in_specs=[
            pl.BlockSpec((2, 1, T, E * ROWS), lambda q: (0, q, 0, 0)),
            pl.BlockSpec((1, T, E * ROWS), lambda q: (q, 0, 0)),
            pl.BlockSpec((E, ROWS, W), lambda q: (0, 0, 0)),
            pl.BlockSpec((E, ROWS, W), lambda q: (0, 0, 0)),
        ],
        out_specs=(pl.BlockSpec((T, W), lambda q: (0, q)), pl.BlockSpec((T, W), lambda q: (0, q))),
    )(pw, pt, bo, bi)

    rows_x = rows_x.reshape(rows, D)
    rows_d = rows_d.reshape(rows, D)
    grad_down = jnp.einsum("rf,rd->fd", hidden, rows_d, preferred_element_type=F32).astype(BF16)
    grad_gate = jnp.einsum("rd,rf->df", rows_x, gate_grad, preferred_element_type=F32).astype(BF16)
    grad_up = jnp.einsum("rd,rf->df", rows_x, up_grad, preferred_element_type=F32).astype(BF16)
    return (mixed, grad_tokens, grad_gate[None], grad_up[None], grad_down[None])


def solution(mesh):
    return jax.shard_map(
        local,
        mesh=mesh,
        in_specs=(
            P(("ep", "blk"), None),
            P(("ep", "blk"), None),
            P(("ep", "blk"), None),
            P(("ep", "blk"), None),
            P("ep", None, "blk"),
            P("ep", None, "blk"),
            P("ep", "blk", None),
        ),
        out_specs=(
            P(("ep", "blk"), None),
            P(("ep", "blk"), None),
            P("ep", None, "blk"),
            P("ep", None, "blk"),
            P("ep", "blk", None),
        ),
        check_vma=False,
    )
```

```python
import functools

import jax
import jax.numpy as jnp
from jax import lax
from jax.experimental import pallas as pl
from jax.experimental.pallas import tpu as pltpu
from jax.sharding import PartitionSpec as P

CAP = 4
CUTS = 4
ROWS = CAP * CUTS
TILE = 256
F32 = jnp.float32
BF16 = jnp.bfloat16
MESH = pl.DeviceIdType.MESH


def mm(a, b):
    return jnp.dot(a, b, preferred_element_type=F32)


def mm_nt(a, b):
    return lax.dot_general(a, b, (((1,), (1,)), ((), ())), preferred_element_type=F32)


def place(shape, row_dim, q):
    row = lax.broadcasted_iota(jnp.int32, shape, row_dim)
    col = lax.broadcasted_iota(jnp.int32, shape, 1 - row_dim)
    hit = (row // CAP) * ROWS + q * CAP + row % CAP == col
    return jnp.where(hit, 1.0, 0.0).astype(BF16)


def routing(route_ref, gates_ref, picked_ref, weight_ref):
    T = route_ref.shape[0]
    shape = picked_ref.shape
    col = lax.broadcasted_iota(jnp.int32, shape, 1)
    member = jnp.zeros(shape, F32)
    weight = jnp.zeros(shape, F32)
    for p in range(route_ref.shape[1]):
        hit = route_ref[:, p : p + 1] == col // CAP
        member += jnp.where(hit, 1.0, 0.0)
        weight += jnp.where(hit, gates_ref[:, p : p + 1], 0.0)
    row_at = lax.broadcasted_iota(jnp.int32, (T, T), 0)
    col_at = lax.broadcasted_iota(jnp.int32, (T, T), 1)
    earlier = jnp.where(col_at < row_at, 1.0, 0.0).astype(BF16)
    places = mm(earlier, member.astype(BF16))
    picked = (member > 0.5) & (jnp.abs(places - (col % CAP).astype(F32)) < 0.5)
    picked_ref[...] = jnp.where(picked, 1.0, 0.0).astype(BF16)
    weight_ref[...] = jnp.where(picked, weight, 0.0)


def exchange(
    E, L, route_ref, gates_ref, tok_hbm, cot_hbm, wg_hbm, wu_hbm, wd_hbm,
    bo_hbm, bi_hbm, xo_hbm, do_hbm, h_ref, a_ref, b_ref, picked_ref, weight_ref,
    pq, sg, tok, cot, wg, wu, wd, xs, ds, xin, din, xg, dg, gp, up,
    yp, ysib, yline, yret, bo, qp, qsib, qline, qret, bi,
    load_sem, out_sem, disp_s, disp_r, gat_s, gat_r, sib_s, sib_r, line_s, line_r, ret_s, ret_r,
):
    ep = lax.axis_index("ep")
    blk = lax.axis_index("blk")
    l = blk // 2
    c = blk % 2
    D = tok.shape[1]
    W = D // CUTS
    R = E * CAP
    rows = 2 * L * R
    sibling = {"blk": 2 * l + (1 - c)}
    right = {"blk": blk + 2}
    left = {"blk": blk - 2}
    has_right = l < L - 1
    has_left = l > 0

    loads = [
        pltpu.make_async_copy(s, d, load_sem.at[i])
        for i, (s, d) in enumerate(
            [(tok_hbm, tok), (cot_hbm, cot), (wg_hbm.at[0], wg), (wu_hbm.at[0], wu), (wd_hbm.at[0], wd)]
        )
    ]
    for cp in loads:
        cp.start()

    barrier = pltpu.get_barrier_semaphore()
    for k in range(1, E):
        pl.semaphore_signal(barrier, inc=1, device_id={"ep": lax.rem(ep + k, E)}, device_id_type=MESH)
    pl.semaphore_signal(barrier, inc=1, device_id=sibling, device_id_type=MESH)

    @pl.when(has_right)
    def _():
        pl.semaphore_signal(barrier, inc=1, device_id=right, device_id_type=MESH)

    @pl.when(has_left)
    def _():
        pl.semaphore_signal(barrier, inc=1, device_id=left, device_id_type=MESH)

    ends = jnp.where(l > 0, 1, 0) + jnp.where(l < L - 1, 1, 0)
    routing(route_ref, gates_ref, picked_ref, weight_ref)
    slot_gate = jnp.sum(weight_ref[...], axis=0, keepdims=True)
    scale = jnp.zeros((E * ROWS, 1), F32)
    for q in range(CUTS):
        at = place((E * ROWS, R), 1, q)
        pq[q] = mm_nt(at, picked_ref[...]).astype(BF16)
        scale += jnp.sum(jnp.where(at > 0, slot_gate, 0.0), axis=1, keepdims=True)
    sg[...] = scale
    pl.semaphore_wait(barrier, E + ends)

    def remote(src, dst, ss, rs, dev):
        return pltpu.make_async_remote_copy(
            src_ref=src, dst_ref=dst, send_sem=ss, recv_sem=rs, device_id=dev, device_id_type=MESH
        )

    tails = []

    def tail(cond, make):
        tails.append((cond, make))

    def ep_copy(n, src, dst, ss, rs, j):
        return remote(src.at[j], dst.at[ep], ss.at[n, j], rs.at[n, ep], {"ep": j})

    def ep_send(n, src, dst, ss, rs):
        for k in range(1, E):
            j = lax.rem(ep + k, E)
            ep_copy(n, src, dst, ss, rs, j).start()
            tail(None, functools.partial(ep_copy, n, src, dst, ss, rs, j))

    def ep_wait(n, src, dst, ss, rs):
        for k in range(1, E):
            j = lax.rem(ep + k, E)
            remote(src.at[j], dst.at[j], ss.at[n, j], rs.at[n, j], {"ep": j}).wait_recv()

    def select(src, dst, own, scale):
        def step(t, carry):
            at = pl.ds(pl.multiple_of(t * TILE, TILE), TILE)
            acc = jnp.zeros((E * ROWS, TILE), F32)
            for q in range(CUTS):
                acc += mm(pq[q], src[:, pl.ds(pl.multiple_of(q * W + t * TILE, TILE), TILE)])
            if scale:
                acc = acc * sg[...]
            dst[:, :, at] = acc.astype(BF16).reshape(E, ROWS, TILE)
            return carry

        lax.fori_loop(0, W // TILE, step, 0)
        own[ep] = dst[ep]

    def settle(src, dst):
        def step(t, carry):
            at = pl.ds(pl.multiple_of(t * TILE, TILE), TILE)
            part = src[:, :, at].reshape(E * ROWS, TILE)
            for q in range(CUTS):
                out = mm(place((R, E * ROWS), 0, q), part)
                col = pl.ds(pl.multiple_of((q % 2) * W + t * TILE, TILE), TILE)
                dst[q // 2, blk, :, col] = out.astype(BF16)
            return carry

        lax.fori_loop(0, W // TILE, step, 0)

    def g_copy(n, buf, j, way, dev):
        b = 2 * j + c
        return remote(buf.at[b], buf.at[b], gat_s.at[n, way, j], gat_r.at[n, b], dev)

    def g_got(n, buf, b):
        remote(buf.at[b], buf.at[b], gat_s.at[n, 0, 0], gat_r.at[n, b], sibling).wait_recv()

    def guarded(cond, fn):
        if cond is None:
            fn()
        else:
            pl.when(cond)(fn)

    def g_send(n, buf, s):
        steps = []
        if s < L - 1:
            steps += [(has_right & (l - s >= 0), l - s, 0, right), (has_left & (l + s < L), l + s, 1, left)]
        if s == 0:
            steps += [(None, l, 2, sibling)]
        else:
            steps += [(l - s >= 0, l - s, 2, sibling), (l + s < L, l + s, 2, sibling)]
        for cond, j, way, dev in steps:
            guarded(cond, lambda j=j, way=way, dev=dev: g_copy(n, buf, j, way, dev).start())
            tail(cond, functools.partial(g_copy, n, buf, j, way, dev))

    def g_wait(n, buf, s):
        pl.when(l - 1 - s >= 0)(lambda: g_got(n, buf, 2 * (l - 1 - s) + c))
        pl.when(l + 1 + s < L)(lambda: g_got(n, buf, 2 * (l + 1 + s) + c))

    def g_sib(n, buf):
        for j in range(L):
            g_got(n, buf, 2 * j + (1 - c))

    def s_copy(n, part, sib, j):
        return remote(part.at[2 * j + 1 - c], sib.at[j], sib_s.at[n, j], sib_r.at[n, j], sibling)

    def s_send(n, part, sib):
        for j in range(L):
            s_copy(n, part, sib, j).start()
            tail(None, functools.partial(s_copy, n, part, sib, j))

    def s_wait(n, part, sib):
        for j in range(L):
            s_copy(n, part, sib, j).wait_recv()

    def r_copy(n, part, line, j, up_way, dev):
        k = j + up_way
        return remote(part.at[2 * j + c], line.at[k], line_s.at[n, j], line_r.at[n, k], dev)

    def total(part, sib, lines, b, j):
        def step(t, carry):
            at = pl.ds(pl.multiple_of(t * 512, 512), 512)
            acc = part[b, :, at].astype(F32) + sib[j, :, at].astype(F32)
            for line, k in lines:
                acc += line[k, :, at].astype(F32)
            part[b, :, at] = acc.astype(BF16)
            return carry

        lax.fori_loop(0, D // 2 // 512, step, 0)

    def r_step(n, part, sib, line, s):
        jl = s - (L - 1 - l)
        jr = L - 1 - s + l

        def go(j, up_way, dev, first):
            def fn():
                if not first:
                    k = j + up_way
                    r_copy(n, part, line, j, up_way, dev).wait_recv()
                    total(part, sib, [(line, k)], 2 * j + c, j)
                else:
                    total(part, sib, [], 2 * j + c, j)
                r_copy(n, part, line, j, up_way, dev).start()

            return fn

        lw = has_left & (jl >= 0)
        rw = has_right & (jr < L)
        pl.when(lw & (l == L - 1))(go(jl, 0, left, True))
        pl.when(rw & (l == 0))(go(jr, 1, right, True))
        if L > 2:
            pl.when(lw & (l < L - 1))(go(jl, 0, left, False))
            pl.when(rw & (l > 0))(go(jr, 1, right, False))
        tail(lw, functools.partial(r_copy, n, part, line, jl, 0, left))
        tail(rw, functools.partial(r_copy, n, part, line, jr, 1, right))

    def r_last(n, part, sib, line, ret, back):
        def join(h, line_slots):
            def fn():
                m = 2 * n + h
                for k in line_slots:
                    remote(
                        part.at[h].at[blk], line.at[h].at[k], line_s.at[m, 0], line_r.at[m, k], sibling
                    ).wait_recv()
                total(part.at[h], sib.at[h], [(line.at[h], k) for k in line_slots], blk, l)

            return fn

        for h in range(2):
            pl.when(l == 0)(join(h, [l]))
            pl.when(l == L - 1)(join(h, [l + 1]))
            if L > 2:
                pl.when((l > 0) & (l < L - 1))(join(h, [l, l + 1]))

        def step(t, carry):
            at = pl.ds(pl.multiple_of(t * TILE, TILE), TILE)
            acc = jnp.zeros((E * ROWS, TILE), F32)
            for q in range(CUTS):
                own = part[q // 2, blk, :, pl.ds(pl.multiple_of((q % 2) * W + t * TILE, TILE), TILE)]
                acc += mm(place((E * ROWS, R), 1, q), own)
            ret[:, :, at] = acc.astype(BF16).reshape(E, ROWS, TILE)
            return carry

        lax.fori_loop(0, W // TILE, step, 0)
        back[ep] = ret[ep]
        ep_send(n, ret, back, ret_s, ret_r)

    def halves(fn, n, *args):
        refs = [r for r in args if not isinstance(r, int)]
        rest = [r for r in args if isinstance(r, int)]
        for h in range(2):
            fn(2 * n + h, *[r.at[h] for r in refs], *rest)

    def pass_on(n, buf, s):
        for h in range(2):
            g_wait(2 * n + h, buf.at[h], s - 1)
            g_send(2 * n + h, buf.at[h], s)

    loads[0].wait()
    select(tok, xs, xin, False)
    ep_send(0, xs, xin, disp_s, disp_r)
    loads[1].wait()
    select(cot, ds, din, True)
    ep_send(1, ds, din, disp_s, disp_r)
    ep_wait(0, xs, xin, disp_s, disp_r)
    settle(xin, xg)
    halves(g_send, 0, xg, 0)
    ep_wait(1, ds, din, disp_s, disp_r)
    settle(din, dg)
    for s in range(1, L):
        pass_on(0, xg, s)
    halves(g_send, 1, dg, 0)
    halves(g_sib, 0, xg)
    x_out = pltpu.make_async_copy(xg, xo_hbm, out_sem.at[0])
    x_out.start()
    loads[2].wait()
    loads[3].wait()

    def quarter(buf, t):
        at = pl.ds(pl.multiple_of((t % 2) * W, TILE), W)
        return buf[t // 2, :, :, at].reshape(rows, W)

    def both(t, carry):
        at = pl.ds(pl.multiple_of(t * W, TILE), W)
        x = quarter(xg, t)
        gp[...] += mm(x, wg[at, :])
        up[...] += mm(x, wu[at, :])
        return carry

    gp[...] = jnp.zeros_like(gp)
    up[...] = jnp.zeros_like(up)
    lax.fori_loop(0, CUTS, both, 0)
    h_ref[...] = (gp[...] * jax.nn.sigmoid(gp[...]) * up[...]).astype(BF16)
    if L > 1:
        pass_on(1, dg, 1)
    loads[4].wait()

    for h in range(2):

        def down(t, carry):
            at = pl.ds(pl.multiple_of(t * 512, 512), 512)
            src = pl.ds(pl.multiple_of(h * (D // 2) + t * 512, 512), 512)
            yp[h, :, :, at] = mm(h_ref[...], wd[:, src]).astype(BF16).reshape(2 * L, R, 512)
            return carry

        lax.fori_loop(0, D // 2 // 512, down, 0)
        s_send(h, yp.at[h], ysib.at[h])
    if L > 2:
        pass_on(1, dg, 2)
    for h in range(2):
        s_wait(h, yp.at[h], ysib.at[h])
        r_step(h, yp.at[h], ysib.at[h], yline.at[h], 0)
    for s in range(3, L):
        pass_on(1, dg, s)
        halves(r_step, 0, yp, ysib, yline, s - 2)
    halves(g_sib, 1, dg)
    d_out = pltpu.make_async_copy(dg, do_hbm, out_sem.at[1])
    d_out.start()

    def pull(t, carry):
        at = pl.ds(pl.multiple_of(t * W, TILE), W)
        return carry + mm_nt(quarter(dg, t), wd[:, at])

    hg = lax.fori_loop(0, CUTS, pull, jnp.zeros((rows, gp.shape[1]), F32))
    g = gp[...]
    u = up[...]
    sig = jax.nn.sigmoid(g)
    a_ref[...] = (hg * u * (sig * (1.0 + g * (1.0 - sig)))).astype(BF16)
    b_ref[...] = (hg * g * sig).astype(BF16)

    for h in range(2):

        def back_rows(t, carry):
            at = pl.ds(pl.multiple_of(t * 512, 512), 512)
            src = pl.ds(pl.multiple_of(h * (D // 2) + t * 512, 512), 512)
            q = mm_nt(a_ref[...], wg[src, :]) + mm_nt(b_ref[...], wu[src, :])
            qp[h, :, :, at] = q.astype(BF16).reshape(2 * L, R, 512)
            return carry

        lax.fori_loop(0, D // 2 // 512, back_rows, 0)
        s_send(2 + h, qp.at[h], qsib.at[h])
    done = max(1, L - 2)
    if done < L - 1:
        halves(r_step, 0, yp, ysib, yline, done)
    for h in range(2):
        s_wait(2 + h, qp.at[h], qsib.at[h])
        r_step(2 + h, qp.at[h], qsib.at[h], qline.at[h], 0)
    r_last(0, yp, ysib, yline, yret, bo)
    for s in range(1, L - 1):
        halves(r_step, 1, qp, qsib, qline, s)
    ep_wait(0, yret, bo, ret_s, ret_r)
    o_out = pltpu.make_async_copy(bo, bo_hbm, out_sem.at[2])
    o_out.start()
    r_last(1, qp, qsib, qline, qret, bi)
    ep_wait(1, qret, bi, ret_s, ret_r)
    i_out = pltpu.make_async_copy(bi, bi_hbm, out_sem.at[3])
    i_out.start()
    for cond, make in tails:
        guarded(cond, lambda make=make: make().wait_send())
    for cp in (x_out, d_out, o_out, i_out):
        cp.wait()


def finish(
    picked_ref, weight_ref, bo_ref, bi_ref, x_ref, d_ref, h_ref, a_ref, b_ref,
    mixed_ref, grad_ref, gg_ref, gu_ref, gd_ref,
):
    q = pl.program_id(0) // 2
    e_rows = bo_ref.shape[0] * ROWS
    width = bo_ref.shape[2]
    rows, F = h_ref.shape
    at = place((picked_ref.shape[1], e_rows), 0, q)
    weight = weight_ref[...]
    hi = weight.astype(BF16)
    lo = (weight - hi.astype(F32)).astype(BF16)
    y = bo_ref[...].reshape(e_rows, width)
    z = bi_ref[...].reshape(e_rows, width)
    mixed = mm(mm(hi, at).astype(BF16), y) + mm(mm(lo, at).astype(BF16), y)
    mixed_ref[...] = mixed.astype(BF16)
    grad_ref[...] = mm(mm(picked_ref[...], at).astype(BF16), z).astype(BF16)
    x_t = x_ref[0].reshape(rows, width).T
    gg_ref[0] = mm(x_t, a_ref[...]).astype(BF16)
    gu_ref[0] = mm(x_t, b_ref[...]).astype(BF16)
    gd_ref[0] = mm(h_ref[...].T, d_ref[0].reshape(rows, width)).astype(BF16)


def local(tokens, route, gates, cotangent, w_gate, w_up, w_down):
    E = lax.axis_size("ep")
    L = lax.axis_size("blk") // 2
    T, D = tokens.shape
    W = D // CUTS
    R = E * CAP
    rows = 2 * L * R
    F = w_gate.shape[2]
    vm = pl.BlockSpec(memory_space=pltpu.VMEM)
    hbm = pl.BlockSpec(memory_space=pl.ANY)
    sds = jax.ShapeDtypeStruct
    msg = pltpu.VMEM((E, ROWS, W), BF16)
    allrows = pltpu.VMEM((2, 2 * L, R, D // 2), BF16)
    own = pltpu.VMEM((2, L, R, D // 2), BF16)
    line = pltpu.VMEM((2, L + 1, R, D // 2), BF16)
    dma = pltpu.SemaphoreType.DMA
    bo, bi, rows_x, rows_d, hidden, gate_grad, up_grad, picked, weight = pl.pallas_call(
        functools.partial(exchange, E, L),
        out_shape=(
            sds((E, ROWS, W), BF16),
            sds((E, ROWS, W), BF16),
            sds((2, 2 * L, R, D // 2), BF16),
            sds((2, 2 * L, R, D // 2), BF16),
            sds((rows, F), BF16),
            sds((rows, F), BF16),
            sds((rows, F), BF16),
            sds((T, R), BF16),
            sds((T, R), F32),
        ),
        in_specs=[vm, vm, hbm, hbm, hbm, hbm, hbm],
        out_specs=(hbm, hbm, hbm, hbm, vm, vm, vm, vm, vm),
        scratch_shapes=[
            pltpu.VMEM((CUTS, E * ROWS, T), BF16),
            pltpu.VMEM((E * ROWS, 1), F32),
            pltpu.VMEM((T, D), BF16),
            pltpu.VMEM((T, D), BF16),
            pltpu.VMEM((D, F), BF16),
            pltpu.VMEM((D, F), BF16),
            pltpu.VMEM((F, D), BF16),
            msg, msg, msg, msg,
            allrows, allrows,
            pltpu.VMEM((rows, F), F32),
            pltpu.VMEM((rows, F), F32),
            allrows, own, line, msg, msg,
            allrows, own, line, msg, msg,
            dma((5,)),
            dma((4,)),
            dma((2, E)),
            dma((2, E)),
            dma((4, 3, L)),
            dma((4, 2 * L)),
            dma((4, L)),
            dma((4, L)),
            dma((4, L)),
            dma((4, L + 1)),
            dma((2, E)),
            dma((2, E)),
        ],
        compiler_params=pltpu.CompilerParams(
            collective_id=0, has_side_effects=True, vmem_limit_bytes=60 * 1024 * 1024
        ),
    )(route, gates, tokens, cotangent, w_gate, w_up, w_down)

    half = W // 2
    whole = lambda j: (0, 0)
    return pl.pallas_call(
        finish,
        grid=(2 * CUTS,),
        out_shape=(
            sds((T, D), BF16),
            sds((T, D), BF16),
            sds((1, D, F), BF16),
            sds((1, D, F), BF16),
            sds((1, F, D), BF16),
        ),
        in_specs=[
            pl.BlockSpec((T, R), whole),
            pl.BlockSpec((T, R), whole),
            pl.BlockSpec((E, ROWS, half), lambda j: (0, 0, j % 2)),
            pl.BlockSpec((E, ROWS, half), lambda j: (0, 0, j % 2)),
            pl.BlockSpec((1, 2 * L, R, half), lambda j: (j // 4, 0, 0, j % 4)),
            pl.BlockSpec((1, 2 * L, R, half), lambda j: (j // 4, 0, 0, j % 4)),
            pl.BlockSpec((rows, F), whole),
            pl.BlockSpec((rows, F), whole),
            pl.BlockSpec((rows, F), whole),
        ],
        out_specs=(
            pl.BlockSpec((T, half), lambda j: (0, j)),
            pl.BlockSpec((T, half), lambda j: (0, j)),
            pl.BlockSpec((1, half, F), lambda j: (0, j, 0)),
            pl.BlockSpec((1, half, F), lambda j: (0, j, 0)),
            pl.BlockSpec((1, F, half), lambda j: (0, 0, j)),
        ),
        compiler_params=pltpu.CompilerParams(vmem_limit_bytes=48 * 1024 * 1024),
    )(picked, weight, bo, bi, rows_x, rows_d, hidden, gate_grad, up_grad)


def solution(mesh):
    return jax.shard_map(
        local,
        mesh=mesh,
        in_specs=(
            P(("ep", "blk"), None),
            P(("ep", "blk"), None),
            P(("ep", "blk"), None),
            P(("ep", "blk"), None),
            P("ep", None, "blk"),
            P("ep", None, "blk"),
            P("ep", "blk", None),
        ),
        out_specs=(
            P(("ep", "blk"), None),
            P(("ep", "blk"), None),
            P("ep", None, "blk"),
            P("ep", None, "blk"),
            P("ep", "blk", None),
        ),
        check_vma=False,
    )
```
